512 devices in a mesh: pipe: 8 (over z), ctx: 64 (over y, x, core).
Axes of the slice: x: 4, y: 8, z: 8, core: 2. Of those that a mesh axis runs over, the one named last changes fastest.
Arguments:
- queries: bfloat16 [8, 8192, 1536], P('pipe', 'ctx'), may hold values from -54 to 54
- keys_values: bfloat16 [8, 8192, 2, 512], P('pipe', 'ctx'), may hold values from -54 to 54
Outputs:
- passed: bfloat16 [8, 8192, 1536], P('pipe', 'ctx')
The draws below stay inside these ranges and needn't reach their ends.
All inputs are finite; a program needn't handle non-finite values.
Results may differ from the reference program's by a relative error of at most 0.006.
Values may be sent and summed in bfloat16 or wider, within the bound.
A program may use at most 64 MiB of HBM per device.

```python
import math
import jax
import jax.numpy as jnp
import numpy as np
from jax import lax

QH = 12
KVH = 4
HD = 128
TOK_DEV = 128
NSEQ = 2
TOKENS = 8192
SECTIONS = 8
N_CTX = 64


def drawn_fields(key):
    base = jax.random.fold_in(key, 7)
    key_q, key_k = jax.random.split(base, 2)
    queries = 1.4 * jnp.clip(jax.random.normal(key_q, (SECTIONS, TOKENS, QH * HD), jnp.float32), -6.0, 6.0)
    pairs = 1.4 * jnp.clip(jax.random.normal(key_k, (SECTIONS, TOKENS, 2, KVH * HD), jnp.float32), -6.0, 6.0)
    return (queries, pairs)


def draw_queries(key, part):
    return drawn_fields(key)[0].astype(jnp.bfloat16)


def draw_keys_values(key, part):
    return drawn_fields(key)[1].astype(jnp.bfloat16)


def setup_inputs(seed: int = 0) -> dict:
    splits = jax.random.split(jax.random.key(seed), 3)
    return {
        "queries": draw_queries(jax.random.fold_in(splits[2], 71), 0),
        "keys_values": draw_keys_values(jax.random.fold_in(splits[2], 71), 0),
    }


def order_rows():
    group = N_CTX // NSEQ
    half = TOK_DEV // 2
    table = np.zeros((NSEQ, TOK_DEV * group), np.int32)
    for seq in range(NSEQ):
        for block in range(2 * group):
            if block < group:
                rank = block
                start = (rank * NSEQ + seq) * TOK_DEV
            else:
                rank = 2 * group - 1 - block
                start = (rank * NSEQ + seq) * TOK_DEV + half
            table[seq, block * half:(block + 1) * half] = np.arange(start, start + half)
    return table

def reference(queries, keys_values):
    table = order_rows()
    flat = table.reshape(-1)
    inverse = np.argsort(flat).astype(np.int32)
    length = table.shape[1]
    share = QH // KVH
    q_all = queries[:, flat].reshape(SECTIONS, NSEQ, length, KVH, share, HD)
    q_all = q_all.transpose(0, 1, 3, 4, 2, 5).reshape(-1, share, length, HD)
    kv_all = keys_values[:, flat].reshape(SECTIONS, NSEQ, length, 2, KVH, HD)
    kv_all = kv_all.transpose(0, 1, 4, 3, 2, 5).reshape(-1, 2, length, HD)
    causal = np.tril(np.ones((length, length), bool))
    scale = 1.0 / math.sqrt(HD)

    def single(item):
        q_block, kv_block = item
        scores = jnp.einsum('gqd,kd->gqk', q_block.astype(jnp.float32), kv_block[0].astype(jnp.float32)) * scale
        scores = jnp.where(causal[None], scores, -1e+30)
        top = lax.optimization_barrier(jnp.max(scores, axis=-1, keepdims=True))
        weights = jnp.exp(scores - top)
        total = lax.optimization_barrier(jnp.sum(weights, axis=-1, keepdims=True))
        rounded = weights.astype(jnp.bfloat16)
        mixed = jnp.einsum('gqk,kd->gqd', rounded.astype(jnp.float32), kv_block[1].astype(jnp.float32))
        return (mixed / total).astype(jnp.bfloat16)
    result = lax.map(single, (q_all, kv_all))
    result = result.reshape(SECTIONS, NSEQ, KVH, share, length, HD).transpose(0, 1, 4, 2, 3, 5)
    result = result.reshape(SECTIONS, NSEQ * length, QH * HD)[:, inverse]
    return jnp.roll(result, 1, axis=0)
```

```python
import functools
import math

import jax
import jax.numpy as jnp
from jax import lax
from jax.experimental import pallas as pl
from jax.experimental.pallas import tpu as pltpu
from jax.sharding import PartitionSpec as P

HD = 128
KVH = 4
SHARE = 3
NSEQ = 2
NX = 4
NY = 8
HALF = 64
BLK = NX * HALF
NEG = -1e30
MESH = pl.DeviceIdType.MESH
A, B = 0, 1


def kernel(q_ref, kv_ref, out_ref, kvs, kvbuf, qbuf, obuf, top, total, acc,
           kv_send, kv_recv, q_send, q_recv, q_own, up_send, up_recv, down_send, down_recv,
           out_send, out_recv):
    pipe = lax.axis_index("pipe")
    ctx = lax.axis_index("ctx")
    core = lax.rem(ctx, NSEQ)
    x = lax.rem(ctx // NSEQ, NX)
    y = ctx // (NSEQ * NX)
    npipe = lax.axis_size("pipe")
    nxt, prv = lax.rem(pipe + 1, npipe), lax.rem(pipe + npipe - 1, npipe)

    def at(px, py):
        return (py * NX + px) * NSEQ + core

    up = (pipe, at(x, lax.rem(y + 1, NY)))
    down = (pipe, at(x, lax.rem(y + NY - 1, NY)))
    peers = [(lax.rem(x + j, NX), lax.rem(x + NX - j, NX)) for j in range(NX)]

    barrier = pltpu.get_barrier_semaphore()

    def greet(device):
        pl.semaphore_signal(barrier, inc=1, device_id=device, device_id_type=MESH)

    for j in range(1, NX):
        greet((pipe, at(peers[j][0], y)))
    greet(up)
    greet(down)
    for j in range(NX):
        greet((prv, at(peers[j][0], y)))

    for i in range(2):
        for part in range(2):
            rows = kv_ref[0, part * HALF:(part + 1) * HALF, i, :]
            for h in range(KVH):
                kvs[h, part, i] = rows[:, h * HD:(h + 1) * HD]

    pl.semaphore_wait(barrier, 2 * NX + 1)

    def place(px, part):
        return (px if part == A else NX - 1 - px) * HALF

    def kv_copy(j, part):
        to, _ = peers[j]
        return pltpu.make_async_remote_copy(
            src_ref=kvs.at[to, part],
            dst_ref=kvbuf.at[y, part, :, pl.ds(pl.multiple_of(place(x, part), HALF), HALF), :],
            send_sem=kv_send.at[j, part], recv_sem=kv_recv.at[j, part],
            device_id=(pipe, at(to, y)), device_id_type=MESH)

    def q_copy(j, part):
        to, _ = peers[j]
        return pltpu.make_async_remote_copy(
            src_ref=q_ref.at[0, pl.ds(part * HALF, HALF), pl.ds(pl.multiple_of(to * SHARE * HD, HD), SHARE * HD)],
            dst_ref=qbuf.at[part, pl.ds(pl.multiple_of(place(x, part), HALF), HALF), :],
            send_sem=q_send.at[j, part], recv_sem=q_recv.at[j, part],
            device_id=(pipe, at(to, y)), device_id_type=MESH)

    def q_local(part):
        return pltpu.make_async_copy(
            q_ref.at[0, pl.ds(part * HALF, HALF), pl.ds(pl.multiple_of(x * SHARE * HD, HD), SHARE * HD)],
            qbuf.at[part, pl.ds(pl.multiple_of(place(x, part), HALF), HALF), :],
            q_own.at[part])

    for part in (A, B):
        for j in (1, 3, 2):
            kv_copy(j, part).start()
    for part in (A, B):
        q_local(part).start()
        for j in (1, 3, 2):
            q_copy(j, part).start()
    for part in (A, B):
        kvbuf[y, part, :, pl.ds(pl.multiple_of(place(x, part), HALF), HALF), :] = kvs[x, part]

    top[...] = jnp.full_like(top, NEG)
    total[...] = jnp.zeros_like(total)
    acc[...] = jnp.zeros_like(acc)

    def ring(upward, part, d):
        owner = lax.rem(y + NY - d, NY) if upward else lax.rem(y + d, NY)
        slot = kvbuf.at[owner, part]
        send, recv = (up_send, up_recv) if upward else (down_send, down_recv)
        return pltpu.make_async_remote_copy(
            src_ref=slot, dst_ref=slot, send_sem=send.at[part, d], recv_sem=recv.at[part, d],
            device_id=up if upward else down, device_id_type=MESH)

    def arrived(upward, part, d):
        owner = lax.rem(y + NY - d, NY) if upward else lax.rem(y + d, NY)
        slot = kvbuf.at[owner, part]
        send, recv = (up_send, up_recv) if upward else (down_send, down_recv)
        pltpu.make_async_remote_copy(
            src_ref=slot, dst_ref=slot, send_sem=send.at[part, d - 1], recv_sem=recv.at[part, d - 1],
            device_id=up if upward else down, device_id_type=MESH).wait_recv()
        return owner

    for part in (A, B):
        for j in (1, 3, 2):
            kv_copy(j, part).wait_recv()
        ring(True, part, 0).start()
        ring(False, part, 0).start()
    for part in (A, B):
        q_local(part).wait()
        for j in (1, 3, 2):
            q_copy(j, part).wait_recv()

    factor = math.log2(math.e) / math.sqrt(HD)

    def attend(rows, owner, part, masked):
        keys, values = kvbuf[owner, part, 0], kvbuf[owner, part, 1]
        for g in range(SHARE):
            q = qbuf[rows, :, g * HD:(g + 1) * HD]
            s = lax.dot_general(keys, q, (((1,), (1,)), ((), ())), preferred_element_type=jnp.float32)
            if masked:
                k_at = lax.broadcasted_iota(jnp.int32, (BLK, BLK), 0)
                q_at = lax.broadcasted_iota(jnp.int32, (BLK, BLK), 1)
                s = jnp.where(k_at <= q_at, s, NEG)
            old = top[rows, g]
            new = jnp.maximum(old, jnp.max(s, axis=0, keepdims=True))
            fade = jnp.exp2((old - new) * factor)
            w = jnp.exp2((s - new) * factor)
            top[rows, g] = new
            total[rows, g] = total[rows, g] * fade + jnp.sum(w, axis=0, keepdims=True)
            acc[rows, g] = acc[rows, g] * fade + lax.dot_general(
                values, w.astype(jnp.bfloat16), (((0,), (0,)), ((), ())), preferred_element_type=jnp.float32)

    def diagonal(rows, _):
        attend(rows, y, rows, True)
        return 0

    lax.fori_loop(0, 2, diagonal, 0)
    attend(B, y, A, False)

    def span(lo, hi, owner, part):
        def one(rows, _):
            attend(rows, owner, part, False)
            return 0
        lax.fori_loop(lo, hi, one, 0)

    def use(owner, part):
        if part == A:
            span(jnp.where(owner < y, 0, 1), 2, owner, A)
        else:
            span(1, jnp.where(owner > y, 2, 1), owner, B)

    def step(d, _):
        for part in (A, B):
            for upward in (True, False):
                owner = arrived(upward, part, d)
                last = 4 if upward == (part == A) else 3

                @pl.when(d < last)
                def _():
                    ring(upward, part, d).start()

                use(owner, part)
        return 0

    lax.fori_loop(1, 4, step, 0)
    use(arrived(True, A, 4), A)
    use(arrived(False, B, 4), B)

    def out_copy(j, part):
        to, _ = peers[j]
        return pltpu.make_async_remote_copy(
            src_ref=obuf.at[part, pl.ds(pl.multiple_of(place(to, part), HALF), HALF), :],
            dst_ref=out_ref.at[0, pl.ds(part * HALF, HALF), pl.ds(pl.multiple_of(x * SHARE * HD, HD), SHARE * HD)],
            send_sem=out_send.at[j, part], recv_sem=out_recv.at[j, part],
            device_id=(nxt, at(to, y)), device_id_type=MESH)

    def out_wait(j, part):
        _, frm = peers[j]
        pltpu.make_async_remote_copy(
            src_ref=obuf.at[part, pl.ds(0, HALF), :],
            dst_ref=out_ref.at[0, pl.ds(part * HALF, HALF), pl.ds(pl.multiple_of(frm * SHARE * HD, HD), SHARE * HD)],
            send_sem=out_send.at[j, part], recv_sem=out_recv.at[j, part],
            device_id=(nxt, at(frm, y)), device_id_type=MESH).wait_recv()

    for part in (A, B):
        for g in range(SHARE):
            o = acc[part, g] / total[part, g]
            obuf[part, :, g * HD:(g + 1) * HD] = o.T.astype(jnp.bfloat16)
        for j in (2, 1, 3, 0):
            out_copy(j, part).start()

    for part in (A, B):
        for j in range(1, NX):
            kv_copy(j, part).wait_send()
            q_copy(j, part).wait_send()
        for d in range(4):
            for upward in (True, False):
                if d < (4 if upward == (part == A) else 3):
                    ring(upward, part, d).wait_send()
        for j in range(NX):
            out_copy(j, part).wait_send()
            out_wait(j, part)


def shards(queries, keys_values):
    dma = pltpu.SemaphoreType.DMA
    return pl.pallas_call(
        kernel,
        out_shape=jax.ShapeDtypeStruct(queries.shape, jnp.bfloat16),
        in_specs=[pl.BlockSpec(memory_space=pl.ANY), pl.BlockSpec(memory_space=pltpu.VMEM)],
        out_specs=pl.BlockSpec(memory_space=pl.ANY),
        scratch_shapes=[
            pltpu.VMEM((KVH, 2, 2, HALF, HD), jnp.bfloat16),
            pltpu.VMEM((NY, 2, 2, BLK, HD), jnp.bfloat16),
            pltpu.VMEM((2, BLK, SHARE * HD), jnp.bfloat16),
            pltpu.VMEM((2, BLK, SHARE * HD), jnp.bfloat16),
            pltpu.VMEM((2, SHARE, 1, BLK), jnp.float32),
            pltpu.VMEM((2, SHARE, 1, BLK), jnp.float32),
            pltpu.VMEM((2, SHARE, HD, BLK), jnp.float32),
            dma((NX, 2)), dma((NX, 2)), dma((NX, 2)), dma((NX, 2)), dma((2,)),
            dma((2, 4)), dma((2, 4)), dma((2, 4)), dma((2, 4)),
            dma((NX, 2)), dma((NX, 2)),
        ],
        compiler_params=pltpu.CompilerParams(
            collective_id=0, has_side_effects=True, vmem_limit_bytes=48 * 1024 * 1024),
        cost_estimate=pl.CostEstimate(flops=3_500_000_000, bytes_accessed=4_000_000, transcendentals=3_400_000),
    )(queries, keys_values)


def solution(mesh):
    placed = (P("pipe", "ctx", None), P("pipe", "ctx", None, None))
    return jax.shard_map(
        shards, mesh=mesh, in_specs=placed, out_specs=P("pipe", "ctx", None), check_vma=False
    )
```

```python
import functools
import math

import jax
import jax.numpy as jnp
from jax import lax
from jax.experimental import pallas as pl
from jax.experimental.pallas import tpu as pltpu
from jax.sharding import PartitionSpec as P

HD = 128
KVH = 4
SHARE = 3
NSEQ = 2
NX = 4
NY = 8
FAR = NY // 2
HALF = 64
BLK = NX * HALF
ROWS = SHARE * BLK
WIDE = SHARE * HD
GO = 2
NEG = -1e30
MESH = pl.DeviceIdType.MESH
A, B = 0, 1


def kernel(q_ref, kv_ref, out_ref, kvin, kvs, kvbuf, qbuf, qs, obuf, top, total, acc,
           load, kv_send, kv_recv, q_send, q_recv, up_send, up_recv, down_send, down_recv,
           out_send, out_recv, go):
    pipe = lax.axis_index("pipe")
    ctx = lax.axis_index("ctx")
    core = lax.rem(ctx, NSEQ)
    x = lax.rem(ctx // NSEQ, NX)
    y = ctx // (NSEQ * NX)
    npipe = lax.axis_size("pipe")
    nxt, prv = lax.rem(pipe + 1, npipe), lax.rem(pipe + npipe - 1, npipe)
    first = core == 1
    in_pipe = jnp.where(first, pipe, nxt)
    out_pipe = jnp.where(first, nxt, pipe)

    def at(px, py):
        return (py * NX + px) * NSEQ + core

    up = (pipe, at(x, lax.rem(y + 1, NY)))
    down = (pipe, at(x, lax.rem(y + NY - 1, NY)))
    twin = (pipe, (y * NX + x) * NSEQ + 1 - core)
    peers = [(lax.rem(x + j, NX), lax.rem(x + NX - j, NX)) for j in range(NX)]

    kv_in = pltpu.make_async_copy(kv_ref.at[0], kvin, load)
    kv_in.start()

    barrier = pltpu.get_barrier_semaphore()

    def greet(device):
        pl.semaphore_signal(barrier, inc=1, device_id=device, device_id_type=MESH)

    for j in range(1, NX):
        greet((pipe, at(peers[j][0], y)))
    greet(up)
    greet(down)
    greet(twin)
    for j in range(NX):
        greet((prv, at(peers[j][0], y)))

    kv_in.wait()
    for i in range(2):
        for part in range(2):
            rows = kvin[part * HALF:(part + 1) * HALF, i, :]
            for h in range(KVH):
                kvs[h, part, i] = rows[:, h * HD:(h + 1) * HD]

    pl.semaphore_wait(barrier, 2 * NX + 2)

    def place(px, part):
        return pl.ds(pl.multiple_of((px if part == A else NX - 1 - px) * HALF, HALF), HALF)

    def head(h):
        return pl.ds(pl.multiple_of(h * WIDE, HD), WIDE)

    def kv_ends(j, part):
        return kvs.at[peers[j][0], part], kvbuf.at[y, part, :, place(x, part), :]

    def q_ends(j, part):
        return q_ref.at[0, pl.ds(part * HALF, HALF), head(peers[j][0])], qbuf.at[part, place(x, part), :]

    def out_ends(j, part):
        return obuf.at[part, place(peers[j][0], part), :], out_ref.at[0, pl.ds(part * HALF, HALF), head(x)]

    def remote(ends, send, recv, j, part, to_pipe):
        src, dst = ends(j, part)
        return pltpu.make_async_remote_copy(
            src_ref=src, dst_ref=dst, send_sem=send.at[j, part], recv_sem=recv.at[j, part],
            device_id=(to_pipe, at(peers[j][0], y)), device_id_type=MESH)

    def local(ends, recv, part):
        src, dst = ends(0, part)
        return pltpu.make_async_copy(src, dst, recv.at[0, part])

    kv_copy = lambda j, part: remote(kv_ends, kv_send, kv_recv, j, part, in_pipe)
    q_copy = lambda j, part: remote(q_ends, q_send, q_recv, j, part, in_pipe)
    out_copy = lambda j, part: remote(out_ends, out_send, out_recv, j, part, out_pipe)

    def begin(copy, ends, recv, part, stays):
        @pl.when(stays)
        def _():
            local(ends, recv, part).start()

        @pl.when(jnp.logical_not(stays))
        def _():
            copy(0, part).start()

        for j in (1, 3, 2):
            copy(j, part).start()

    def landed(copy, ends, recv, j, part, stays):
        if j > 0:
            copy(j, part).wait_recv()
            return

        @pl.when(stays)
        def _():
            local(ends, recv, part).wait()

        @pl.when(jnp.logical_not(stays))
        def _():
            copy(0, part).wait_recv()

    def sent(copy, part, stays):
        @pl.when(jnp.logical_not(stays))
        def _():
            copy(0, part).wait_send()

        for j in (1, 3, 2):
            copy(j, part).wait_send()

    begin(kv_copy, kv_ends, kv_recv, A, first)
    begin(kv_copy, kv_ends, kv_recv, B, first)
    begin(q_copy, q_ends, q_recv, A, first)
    begin(q_copy, q_ends, q_recv, B, first)

    top[...] = jnp.full_like(top, NEG)
    total[...] = jnp.zeros_like(total)
    acc[...] = jnp.zeros_like(acc)

    def owner_of(upward, d):
        return lax.rem(y + NY - d, NY) if upward else lax.rem(y + d, NY)

    def ring(upward, part, d):
        slot = kvbuf.at[owner_of(upward, d), part]
        send, recv = (up_send, up_recv) if upward else (down_send, down_recv)
        return pltpu.make_async_remote_copy(
            src_ref=slot, dst_ref=slot, send_sem=send.at[part, d], recv_sem=recv.at[part, d],
            device_id=up if upward else down, device_id_type=MESH)

    def needed(upward, part, d):
        hops = FAR if upward == (part == A) else FAR - 1
        ok = d < hops
        if part == B:
            owner = owner_of(upward, d)
            ok = jnp.logical_and(ok, owner + FAR - 1 >= NY if upward else owner - d - 1 >= 0)
        return ok

    def pass_on(upward, part, d):
        @pl.when(needed(upward, part, d))
        def _():
            ring(upward, part, d).start()

    def arrive(upward, part, d):
        owner = owner_of(upward, d)
        ok = True if part == A else (owner + FAR - 1 >= NY if upward else y + d < NY)
        slot = kvbuf.at[owner, part]
        send, recv = (up_send, up_recv) if upward else (down_send, down_recv)

        @pl.when(ok)
        def _():
            pltpu.make_async_remote_copy(
                src_ref=slot, dst_ref=slot, send_sem=send.at[part, d - 1], recv_sem=recv.at[part, d - 1],
                device_id=up if upward else down, device_id_type=MESH).wait_recv()

        pass_on(upward, part, d)

    last_plane = pipe == npipe - 1

    @pl.when(jnp.logical_and(last_plane, jnp.logical_not(first)))
    def _():
        pl.semaphore_wait(go, 1)

    for part, j in ((A, 0), (B, 0), (A, 1), (A, 3), (A, 2), (B, 1), (B, 3), (B, 2)):
        landed(kv_copy, kv_ends, kv_recv, j, part, first)
        piece = kvbuf.at[y, part, :, place(peers[j][1], part), :]
        for upward in (True, False):
            @pl.when(needed(upward, part, 0))
            def _():
                pltpu.make_async_remote_copy(
                    src_ref=piece, dst_ref=piece,
                    send_sem=(up_send if upward else down_send).at[part, 0],
                    recv_sem=(up_recv if upward else down_recv).at[part, 0],
                    device_id=up if upward else down, device_id_type=MESH).start()

    for part in (A, B):
        for j in range(NX):
            landed(q_copy, q_ends, q_recv, j, part, first)
        for g in range(SHARE):
            qs[part, g * BLK:(g + 1) * BLK, :] = qbuf[part, :, g * HD:(g + 1) * HD]

    factor = math.log2(math.e) / math.sqrt(HD)

    def attend(rows, blocks, shift=None):
        keys = jnp.concatenate([kvbuf[o, p, 0] for o, p in blocks], axis=0)
        values = jnp.concatenate([kvbuf[o, p, 1] for o, p in blocks], axis=0)
        count = len(blocks) * BLK
        s = lax.dot_general(qs[rows], keys, (((1,), (1,)), ((), ())), preferred_element_type=jnp.float32)
        if shift is not None:
            q_at = lax.broadcasted_iota(jnp.int32, (SHARE, BLK, count), 1).reshape(ROWS, count)
            k_at = lax.broadcasted_iota(jnp.int32, (ROWS, count), 1)
            s = jnp.where(k_at <= q_at + shift, s, NEG)
        old = top[rows]
        new = jnp.maximum(old, jnp.max(s, axis=1, keepdims=True))
        fade = jnp.exp2((old - new) * factor)
        w = jnp.exp2((s - jnp.concatenate([new] * (count // HD), axis=1)) * factor)
        top[rows] = new
        total[rows] = total[rows] * fade + jnp.sum(w, axis=1, keepdims=True)
        acc[rows] = acc[rows] * fade + jnp.dot(w.astype(jnp.bfloat16), values, preferred_element_type=jnp.float32)

    attend(A, [(y, A)], 0)
    attend(B, [(y, A), (y, B)], BLK)

    def same(d):
        for upward in (True, False):
            owner = owner_of(upward, d)
            part = jnp.where(owner < y, A, B)
            attend(part, [(owner, part)])

    def step(d, _):
        arrive(True, A, d)
        arrive(False, A, d)

        @pl.when(d > 1)
        def _():
            same(d - 1)

        arrive(True, B, d)
        arrive(False, B, d)

        @pl.when(jnp.logical_and(d == GO, jnp.logical_and(last_plane, first)))
        def _():
            pl.semaphore_signal(go, inc=1, device_id=twin, device_id_type=MESH)

        attend(B, [(owner_of(True, d), A), (owner_of(False, d), A)])
        return 0

    lax.fori_loop(1, FAR, step, 0)
    same(FAR - 1)
    arrive(True, A, FAR)
    far = owner_of(True, FAR)

    @pl.when(far < y)
    def _():
        attend(A, [(far, A)])

    def finish(part):
        o = acc[part] / total[part]
        for g in range(SHARE):
            obuf[part, :, g * HD:(g + 1) * HD] = o[g * BLK:(g + 1) * BLK].astype(jnp.bfloat16)
        begin(out_copy, out_ends, out_recv, part, jnp.logical_not(first))

    finish(A)
    arrive(False, B, FAR)

    @pl.when(far < y)
    def _():
        attend(B, [(far, A)])

    @pl.when(far > y)
    def _():
        attend(B, [(far, A), (far, B)])

    finish(B)

    for part in (A, B):
        sent(kv_copy, part, first)
        sent(q_copy, part, first)
        for d in range(FAR):
            for upward in (True, False):
                @pl.when(needed(upward, part, d))
                def _():
                    ring(upward, part, d).wait_send()
        sent(out_copy, part, jnp.logical_not(first))

    for part in (A, B):
        @pl.when(jnp.logical_not(first))
        def _():
            local(out_ends, out_recv, part).wait()

        for j in range(NX):
            def came():
                dst = out_ref.at[0, pl.ds(part * HALF, HALF), head(peers[j][1])]
                pltpu.make_async_remote_copy(
                    src_ref=obuf.at[part, pl.ds(0, HALF), :], dst_ref=dst,
                    send_sem=out_send.at[j, part], recv_sem=out_recv.at[j, part],
                    device_id=(out_pipe, at(peers[j][1], y)), device_id_type=MESH).wait_recv()

            if j == 0:
                pl.when(first)(came)
            else:
                came()


def shards(queries, keys_values):
    dma = pltpu.SemaphoreType.DMA
    bf16, f32 = jnp.bfloat16, jnp.float32
    return pl.pallas_call(
        kernel,
        out_shape=jax.ShapeDtypeStruct(queries.shape, bf16),
        in_specs=[pl.BlockSpec(memory_space=pltpu.HBM), pl.BlockSpec(memory_space=pltpu.HBM)],
        out_specs=pl.BlockSpec(memory_space=pl.ANY),
        scratch_shapes=[
            pltpu.VMEM(keys_values.shape[1:], bf16),
            pltpu.VMEM((KVH, 2, 2, HALF, HD), bf16),
            pltpu.VMEM((NY, 2, 2, BLK, HD), bf16),
            pltpu.VMEM((2, BLK, WIDE), bf16),
            pltpu.VMEM((2, ROWS, HD), bf16),
            pltpu.VMEM((2, BLK, WIDE), bf16),
            pltpu.VMEM((2, ROWS, HD), f32),
            pltpu.VMEM((2, ROWS, HD), f32),
            pltpu.VMEM((2, ROWS, HD), f32),
            dma, dma((NX, 2)), dma((NX, 2)), dma((NX, 2)), dma((NX, 2)),
            dma((2, FAR)), dma((2, FAR)), dma((2, FAR)), dma((2, FAR)),
            dma((NX, 2)), dma((NX, 2)), pltpu.SemaphoreType.REGULAR,
        ],
        compiler_params=pltpu.CompilerParams(
            collective_id=0, has_side_effects=True, vmem_limit_bytes=62 * 1024 * 1024),
        cost_estimate=pl.CostEstimate(flops=3_500_000_000, bytes_accessed=4_000_000, transcendentals=3_400_000),
    )(queries, keys_values)


def solution(mesh):
    placed = (P("pipe", "ctx", None), P("pipe", "ctx", None, None))
    return jax.shard_map(
        shards, mesh=mesh, in_specs=placed, out_specs=P("pipe", "ctx", None), check_vma=False
    )
```

```python
import functools
import math

import jax
import jax.numpy as jnp
from jax import lax
from jax.experimental import pallas as pl
from jax.experimental.pallas import tpu as pltpu
from jax.sharding import PartitionSpec as P

HD = 128
KVH = 4
SHARE = 3
NSEQ = 2
NX = 4
NY = 8
FAR = NY // 2
CUTS = 2
HALF = 64
BLK = NX * HALF
ROWS = SHARE * BLK
CUT = BLK // CUTS
WIDE = SHARE * HD
GO = 2
NEG = -1e30
MESH = pl.DeviceIdType.MESH
A, B = 0, 1


def kernel(q_ref, kv_ref, out_ref, kvin, kvs, kvbuf, qbuf, qs, obuf, top, total, acc,
           load, kv_send, kv_recv, q_send, q_recv, up_send, up_recv, down_send, down_recv,
           out_send, out_recv, go):
    pipe = lax.axis_index("pipe")
    ctx = lax.axis_index("ctx")
    core = lax.rem(ctx, NSEQ)
    x = lax.rem(ctx // NSEQ, NX)
    y = ctx // (NSEQ * NX)
    npipe = lax.axis_size("pipe")
    nxt, prv = lax.rem(pipe + 1, npipe), lax.rem(pipe + npipe - 1, npipe)
    first = core == 1
    in_pipe = jnp.where(first, pipe, nxt)
    out_pipe = jnp.where(first, nxt, pipe)

    def at(px, py):
        return (py * NX + px) * NSEQ + core

    up = (pipe, at(x, lax.rem(y + 1, NY)))
    down = (pipe, at(x, lax.rem(y + NY - 1, NY)))
    twin = (pipe, (y * NX + x) * NSEQ + 1 - core)
    peers = [(lax.rem(x + j, NX), lax.rem(x + NX - j, NX)) for j in range(NX)]

    kv_in = pltpu.make_async_copy(kv_ref.at[0], kvin, load)
    kv_in.start()

    barrier = pltpu.get_barrier_semaphore()

    def greet(device):
        pl.semaphore_signal(barrier, inc=1, device_id=device, device_id_type=MESH)

    for j in range(1, NX):
        greet((pipe, at(peers[j][0], y)))
    greet(up)
    greet(down)
    greet(twin)
    for j in range(NX):
        greet((prv, at(peers[j][0], y)))

    def separate(part):
        for i in range(2):
            rows = kvin[part * HALF:(part + 1) * HALF, i, :]
            for h in range(KVH):
                kvs[h, part, i] = rows[:, h * HD:(h + 1) * HD]

    kv_in.wait()
    separate(A)
    pl.semaphore_wait(barrier, 2 * NX + 2)

    def place(px, part):
        return pl.ds(pl.multiple_of((px if part == A else NX - 1 - px) * HALF, HALF), HALF)

    def head(h):
        return pl.ds(pl.multiple_of(h * WIDE, HD), WIDE)

    def kv_ends(j, part):
        return kvs.at[peers[j][0], part], kvbuf.at[y, part, :, place(x, part), :]

    def q_ends(j, part):
        return q_ref.at[0, pl.ds(part * HALF, HALF), head(peers[j][0])], qbuf.at[part, place(x, part), :]

    def out_ends(j, part):
        return obuf.at[part, place(peers[j][0], part), :], out_ref.at[0, pl.ds(part * HALF, HALF), head(x)]

    def remote(ends, send, recv, j, part, to_pipe):
        src, dst = ends(j, part)
        return pltpu.make_async_remote_copy(
            src_ref=src, dst_ref=dst, send_sem=send.at[j, part], recv_sem=recv.at[j, part],
            device_id=(to_pipe, at(peers[j][0], y)), device_id_type=MESH)

    def local(ends, recv, part):
        src, dst = ends(0, part)
        return pltpu.make_async_copy(src, dst, recv.at[0, part])

    kv_copy = lambda j, part: remote(kv_ends, kv_send, kv_recv, j, part, in_pipe)
    q_copy = lambda j, part: remote(q_ends, q_send, q_recv, j, part, in_pipe)
    out_copy = lambda j, part: remote(out_ends, out_send, out_recv, j, part, out_pipe)

    def begin(copy, ends, recv, part, stays):
        @pl.when(stays)
        def _():
            local(ends, recv, part).start()

        @pl.when(jnp.logical_not(stays))
        def _():
            copy(0, part).start()

        for j in (1, 3, 2):
            copy(j, part).start()

    def landed(copy, ends, recv, j, part, stays):
        if j > 0:
            copy(j, part).wait_recv()
            return

        @pl.when(stays)
        def _():
            local(ends, recv, part).wait()

        @pl.when(jnp.logical_not(stays))
        def _():
            copy(0, part).wait_recv()

    def sent(copy, part, stays):
        @pl.when(jnp.logical_not(stays))
        def _():
            copy(0, part).wait_send()

        for j in (1, 3, 2):
            copy(j, part).wait_send()

    begin(kv_copy, kv_ends, kv_recv, A, first)
    separate(B)
    begin(kv_copy, kv_ends, kv_recv, B, first)
    begin(q_copy, q_ends, q_recv, A, first)
    begin(q_copy, q_ends, q_recv, B, first)

    top[...] = jnp.full_like(top, NEG)
    total[...] = jnp.zeros_like(total)
    acc[...] = jnp.zeros_like(acc)

    def owner_of(upward, d):
        return lax.rem(y + NY - d, NY) if upward else lax.rem(y + d, NY)

    def ring(upward, part, d, cut):
        slot = kvbuf.at[owner_of(upward, d), part, :, pl.ds(cut * CUT, CUT), :]
        send, recv = (up_send, up_recv) if upward else (down_send, down_recv)
        return pltpu.make_async_remote_copy(
            src_ref=slot, dst_ref=slot, send_sem=send.at[part, d, cut], recv_sem=recv.at[part, d, cut],
            device_id=up if upward else down, device_id_type=MESH)

    def needed(upward, part, d):
        hops = FAR if upward == (part == A) else FAR - 1
        ok = d < hops
        if part == B:
            owner = owner_of(upward, d)
            ok = jnp.logical_and(ok, owner + FAR - 1 >= NY if upward else owner - d - 1 >= 0)
        return ok

    def arrive(upward, part, d, cut):
        owner = owner_of(upward, d)
        ok = True if part == A else (owner + FAR - 1 >= NY if upward else y + d < NY)
        slot = kvbuf.at[owner, part, :, pl.ds(cut * CUT, CUT), :]
        send, recv = (up_send, up_recv) if upward else (down_send, down_recv)

        @pl.when(ok)
        def _():
            pltpu.make_async_remote_copy(
                src_ref=slot, dst_ref=slot, send_sem=send.at[part, d - 1, cut], recv_sem=recv.at[part, d - 1, cut],
                device_id=up if upward else down, device_id_type=MESH).wait_recv()

        @pl.when(needed(upward, part, d))
        def _():
            ring(upward, part, d, cut).start()

    last_plane = pipe == npipe - 1

    @pl.when(jnp.logical_and(last_plane, jnp.logical_not(first)))
    def _():
        pl.semaphore_wait(go, 1)

    for part, j in ((A, 0), (B, 0), (A, 1), (A, 3), (A, 2), (B, 1), (B, 3), (B, 2)):
        landed(kv_copy, kv_ends, kv_recv, j, part, first)
        frm = peers[j][1]
        piece = kvbuf.at[y, part, :, place(frm, part), :]
        cut = (frm if part == A else NX - 1 - frm) // (NX // CUTS)
        for upward in (True, False):
            @pl.when(needed(upward, part, 0))
            def _():
                pltpu.make_async_remote_copy(
                    src_ref=piece, dst_ref=piece,
                    send_sem=(up_send if upward else down_send).at[part, 0, cut],
                    recv_sem=(up_recv if upward else down_recv).at[part, 0, cut],
                    device_id=up if upward else down, device_id_type=MESH).start()

    factor = math.log2(math.e) / math.sqrt(HD)

    def attend(rows, blocks, shift=None):
        keys = jnp.concatenate([kvbuf[o, p, 0] for o, p in blocks], axis=0)
        values = jnp.concatenate([kvbuf[o, p, 1] for o, p in blocks], axis=0)
        count = len(blocks) * BLK
        s = lax.dot_general(qs[rows], keys, (((1,), (1,)), ((), ())), preferred_element_type=jnp.float32)
        if shift is not None:
            q_at = lax.broadcasted_iota(jnp.int32, (SHARE, BLK, count), 1).reshape(ROWS, count)
            k_at = lax.broadcasted_iota(jnp.int32, (ROWS, count), 1)
            s = jnp.where(k_at <= q_at + shift, s, NEG)
        old = top[rows]
        new = jnp.maximum(old, jnp.max(s, axis=1, keepdims=True))
        fade = jnp.exp2((old - new) * factor)
        w = jnp.exp2((s - jnp.concatenate([new] * (count // HD), axis=1)) * factor)
        top[rows] = new
        total[rows] = total[rows] * fade + jnp.sum(w, axis=1, keepdims=True)
        acc[rows] = acc[rows] * fade + jnp.dot(w.astype(jnp.bfloat16), values, preferred_element_type=jnp.float32)

    def same(d):
        for upward in (True, False):
            owner = owner_of(upward, d)
            part = jnp.where(owner < y, A, B)
            attend(part, [(owner, part)])

    def late(d):
        attend(B, [(owner_of(True, d), A), (owner_of(False, d), A)])

    def both(part, d):
        for cut in range(CUTS):
            arrive(True, part, d, cut)
            arrive(False, part, d, cut)

        @pl.when(jnp.logical_and(jnp.logical_and(d == GO, part == B), jnp.logical_and(last_plane, first)))
        def _():
            pl.semaphore_signal(go, inc=1, device_id=twin, device_id_type=MESH)

    both(A, 1)
    both(B, 1)

    for part in (A, B):
        for j in range(NX):
            landed(q_copy, q_ends, q_recv, j, part, first)
        for g in range(SHARE):
            qs[part, g * BLK:(g + 1) * BLK, :] = qbuf[part, :, g * HD:(g + 1) * HD]

    attend(A, [(y, A)], 0)
    attend(B, [(y, A), (y, B)], BLK)

    def step(d, _):
        both(A, d)
        late(d - 1)
        both(B, d)
        same(d - 1)
        return 0

    lax.fori_loop(2, FAR, step, 0)
    late(FAR - 1)
    same(FAR - 1)
    for cut in range(CUTS):
        arrive(True, A, FAR, cut)
    far = owner_of(True, FAR)

    @pl.when(far < y)
    def _():
        attend(A, [(far, A)])

    def finish(part):
        o = acc[part] / total[part]
        for g in range(SHARE):
            obuf[part, :, g * HD:(g + 1) * HD] = o[g * BLK:(g + 1) * BLK].astype(jnp.bfloat16)
        begin(out_copy, out_ends, out_recv, part, jnp.logical_not(first))

    finish(A)
    for cut in range(CUTS):
        arrive(False, B, FAR, cut)

    @pl.when(far < y)
    def _():
        attend(B, [(far, A)])

    @pl.when(far > y)
    def _():
        attend(B, [(far, A), (far, B)])

    finish(B)

    for part in (A, B):
        sent(kv_copy, part, first)
        sent(q_copy, part, first)
        for d in range(FAR):
            for upward in (True, False):
                @pl.when(needed(upward, part, d))
                def _():
                    for cut in range(CUTS):
                        ring(upward, part, d, cut).wait_send()
        sent(out_copy, part, jnp.logical_not(first))

    for part in (A, B):
        @pl.when(jnp.logical_not(first))
        def _():
            local(out_ends, out_recv, part).wait()

        for j in range(NX):
            def came():
                dst = out_ref.at[0, pl.ds(part * HALF, HALF), head(peers[j][1])]
                pltpu.make_async_remote_copy(
                    src_ref=obuf.at[part, pl.ds(0, HALF), :], dst_ref=dst,
                    send_sem=out_send.at[j, part], recv_sem=out_recv.at[j, part],
                    device_id=(out_pipe, at(peers[j][1], y)), device_id_type=MESH).wait_recv()

            if j == 0:
                pl.when(first)(came)
            else:
                came()


def shards(queries, keys_values):
    dma = pltpu.SemaphoreType.DMA
    bf16, f32 = jnp.bfloat16, jnp.float32
    return pl.pallas_call(
        kernel,
        out_shape=pltpu.VMEM(queries.shape, bf16),
        in_specs=[pl.BlockSpec(memory_space=pltpu.HBM), pl.BlockSpec(memory_space=pltpu.HBM)],
        out_specs=pl.BlockSpec(memory_space=pl.ANY),
        scratch_shapes=[
            pltpu.VMEM(keys_values.shape[1:], bf16),
            pltpu.VMEM((KVH, 2, 2, HALF, HD), bf16),
            pltpu.VMEM((NY, 2, 2, BLK, HD), bf16),
            pltpu.VMEM((2, BLK, WIDE), bf16),
            pltpu.VMEM((2, ROWS, HD), bf16),
            pltpu.VMEM((2, BLK, WIDE), bf16),
            pltpu.VMEM((2, ROWS, HD), f32),
            pltpu.VMEM((2, ROWS, HD), f32),
            pltpu.VMEM((2, ROWS, HD), f32),
            dma, dma((NX, 2)), dma((NX, 2)), dma((NX, 2)), dma((NX, 2)),
            dma((2, FAR, CUTS)), dma((2, FAR, CUTS)), dma((2, FAR, CUTS)), dma((2, FAR, CUTS)),
            dma((NX, 2)), dma((NX, 2)), pltpu.SemaphoreType.REGULAR,
        ],
        compiler_params=pltpu.CompilerParams(
            collective_id=0, has_side_effects=True, vmem_limit_bytes=48 * 1024 * 1024),
        cost_estimate=pl.CostEstimate(flops=3_500_000_000, bytes_accessed=4_000_000, transcendentals=3_400_000),
    )(pltpu.with_memory_space_constraint(queries, pltpu.HBM), pltpu.with_memory_space_constraint(keys_values, pltpu.HBM))


def solution(mesh):
    placed = (P("pipe", "ctx", None), P("pipe", "ctx", None, None))
    return jax.shard_map(
        shards, mesh=mesh, in_specs=placed, out_specs=P("pipe", "ctx", None), check_vma=False
    )
```

```python
import functools
import math

import jax
import jax.numpy as jnp
from jax import lax
from jax.experimental import pallas as pl
from jax.experimental.pallas import tpu as pltpu
from jax.sharding import PartitionSpec as P

HD = 128
KVH = 4
SHARE = 3
NSEQ = 2
NX = 4
NY = 8
FAR = NY // 2
CUTS = 2
HALF = 64
BLK = NX * HALF
ROWS = SHARE * BLK
CUT = BLK // CUTS
WIDE = SHARE * HD
GO = 2
NEG = -1e30
MESH = pl.DeviceIdType.MESH
A, B = 0, 1


def kernel(q_ref, kv_ref, out_ref, kvin, kvs, kvbuf, qbuf, qs, obuf, top, total, acc,
           load, kv_send, kv_recv, q_send, q_recv, up_send, up_recv, down_send, down_recv,
           out_send, out_recv, go):
    pipe = lax.axis_index("pipe")
    ctx = lax.axis_index("ctx")
    core = lax.rem(ctx, NSEQ)
    x = lax.rem(ctx // NSEQ, NX)
    y = ctx // (NSEQ * NX)
    npipe = lax.axis_size("pipe")
    nxt, prv = lax.rem(pipe + 1, npipe), lax.rem(pipe + npipe - 1, npipe)
    first = core == 1
    in_pipe = jnp.where(first, pipe, nxt)
    out_pipe = jnp.where(first, nxt, pipe)

    def at(px, py):
        return (py * NX + px) * NSEQ + core

    up = (pipe, at(x, lax.rem(y + 1, NY)))
    down = (pipe, at(x, lax.rem(y + NY - 1, NY)))
    twin = (pipe, (y * NX + x) * NSEQ + 1 - core)
    peers = [(lax.rem(x + j, NX), lax.rem(x + NX - j, NX)) for j in range(NX)]

    kv_in = pltpu.make_async_copy(kv_ref.at[0], kvin, load)
    kv_in.start()

    barrier = pltpu.get_barrier_semaphore()

    def greet(device):
        pl.semaphore_signal(barrier, inc=1, device_id=device, device_id_type=MESH)

    for j in range(1, NX):
        greet((pipe, at(peers[j][0], y)))
    greet(up)
    greet(down)
    greet(twin)
    for j in range(NX):
        greet((prv, at(peers[j][0], y)))

    def separate(part):
        for i in range(2):
            rows = kvin[part * HALF:(part + 1) * HALF, i, :]
            for h in range(KVH):
                kvs[h, part, i] = rows[:, h * HD:(h + 1) * HD]

    kv_in.wait()
    separate(A)
    pl.semaphore_wait(barrier, 2 * NX + 2)

    def place(px, part):
        return pl.ds(pl.multiple_of((px if part == A else NX - 1 - px) * HALF, HALF), HALF)

    def head(h):
        return pl.ds(pl.multiple_of(h * WIDE, HD), WIDE)

    def kv_ends(j, part):
        return kvs.at[peers[j][0], part], kvbuf.at[y, part, :, place(x, part), :]

    def q_ends(j, part):
        return q_ref.at[0, pl.ds(part * HALF, HALF), head(peers[j][0])], qbuf.at[part, place(x, part), :]

    def out_ends(j, part):
        return obuf.at[part, place(peers[j][0], part), :], out_ref.at[0, pl.ds(part * HALF, HALF), head(x)]

    def remote(ends, send, recv, j, part, to_pipe):
        src, dst = ends(j, part)
        return pltpu.make_async_remote_copy(
            src_ref=src, dst_ref=dst, send_sem=send.at[j, part], recv_sem=recv.at[j, part],
            device_id=(to_pipe, at(peers[j][0], y)), device_id_type=MESH)

    def local(ends, recv, part):
        src, dst = ends(0, part)
        return pltpu.make_async_copy(src, dst, recv.at[0, part])

    kv_copy = lambda j, part: remote(kv_ends, kv_send, kv_recv, j, part, in_pipe)
    q_copy = lambda j, part: remote(q_ends, q_send, q_recv, j, part, in_pipe)
    out_copy = lambda j, part: remote(out_ends, out_send, out_recv, j, part, out_pipe)

    def begin(copy, ends, recv, part, stays):
        @pl.when(stays)
        def _():
            local(ends, recv, part).start()

        @pl.when(jnp.logical_not(stays))
        def _():
            copy(0, part).start()

        for j in (1, 3, 2):
            copy(j, part).start()

    def landed(copy, ends, recv, j, part, stays):
        if j > 0:
            copy(j, part).wait_recv()
            return

        @pl.when(stays)
        def _():
            local(ends, recv, part).wait()

        @pl.when(jnp.logical_not(stays))
        def _():
            copy(0, part).wait_recv()

    def sent(copy, part, stays):
        @pl.when(jnp.logical_not(stays))
        def _():
            copy(0, part).wait_send()

        for j in (1, 3, 2):
            copy(j, part).wait_send()

    begin(kv_copy, kv_ends, kv_recv, A, first)
    separate(B)
    begin(kv_copy, kv_ends, kv_recv, B, first)
    begin(q_copy, q_ends, q_recv, A, first)
    begin(q_copy, q_ends, q_recv, B, first)

    top[...] = jnp.full_like(top, NEG)
    total[...] = jnp.zeros_like(total)
    acc[...] = jnp.zeros_like(acc)

    def owner_of(upward, d):
        return lax.rem(y + NY - d, NY) if upward else lax.rem(y + d, NY)

    def ring(upward, part, d, cut):
        slot = kvbuf.at[owner_of(upward, d), part, :, pl.ds(cut * CUT, CUT), :]
        send, recv = (up_send, up_recv) if upward else (down_send, down_recv)
        return pltpu.make_async_remote_copy(
            src_ref=slot, dst_ref=slot, send_sem=send.at[part, d, cut], recv_sem=recv.at[part, d, cut],
            device_id=up if upward else down, device_id_type=MESH)

    def travels(upward, part, owner, d):
        if part == A:
            return d <= (FAR if upward else FAR - 1)
        if upward:
            return jnp.logical_and(owner > FAR, d <= FAR)
        return jnp.logical_and(owner >= d, d <= jnp.where(owner == FAR, FAR, FAR - 1))

    def needed(upward, part, d):
        return travels(upward, part, owner_of(upward, d), d + 1)

    def arrive(upward, part, d, cut):
        owner = owner_of(upward, d)
        slot = kvbuf.at[owner, part, :, pl.ds(cut * CUT, CUT), :]
        send, recv = (up_send, up_recv) if upward else (down_send, down_recv)

        @pl.when(travels(upward, part, owner, d))
        def _():
            pltpu.make_async_remote_copy(
                src_ref=slot, dst_ref=slot, send_sem=send.at[part, d - 1, cut], recv_sem=recv.at[part, d - 1, cut],
                device_id=up if upward else down, device_id_type=MESH).wait_recv()

        @pl.when(needed(upward, part, d))
        def _():
            ring(upward, part, d, cut).start()

    last_plane = pipe == npipe - 1

    @pl.when(jnp.logical_and(last_plane, jnp.logical_not(first)))
    def _():
        pl.semaphore_wait(go, 1)

    for part, j in ((A, 0), (B, 0), (A, 1), (A, 3), (A, 2), (B, 1), (B, 3), (B, 2)):
        landed(kv_copy, kv_ends, kv_recv, j, part, first)
        frm = peers[j][1]
        piece = kvbuf.at[y, part, :, place(frm, part), :]
        cut = (frm if part == A else NX - 1 - frm) // (NX // CUTS)
        for upward in (True, False):
            @pl.when(needed(upward, part, 0))
            def _():
                pltpu.make_async_remote_copy(
                    src_ref=piece, dst_ref=piece,
                    send_sem=(up_send if upward else down_send).at[part, 0, cut],
                    recv_sem=(up_recv if upward else down_recv).at[part, 0, cut],
                    device_id=up if upward else down, device_id_type=MESH).start()

    factor = math.log2(math.e) / math.sqrt(HD)

    def attend(rows, blocks, shift=None):
        keys = jnp.concatenate([kvbuf[o, p, 0] for o, p in blocks], axis=0)
        values = jnp.concatenate([kvbuf[o, p, 1] for o, p in blocks], axis=0)
        count = len(blocks) * BLK
        s = lax.dot_general(qs[rows], keys, (((1,), (1,)), ((), ())), preferred_element_type=jnp.float32)
        if shift is not None:
            q_at = lax.broadcasted_iota(jnp.int32, (SHARE, BLK, count), 1).reshape(ROWS, count)
            k_at = lax.broadcasted_iota(jnp.int32, (ROWS, count), 1)
            s = jnp.where(k_at <= q_at + shift, s, NEG)
        old = top[rows]
        new = jnp.maximum(old, jnp.max(s, axis=1, keepdims=True))
        fade = jnp.exp2((old - new) * factor)
        w = jnp.exp2((s - jnp.concatenate([new] * (count // HD), axis=1)) * factor)
        top[rows] = new
        total[rows] = total[rows] * fade + jnp.sum(w, axis=1, keepdims=True)
        acc[rows] = acc[rows] * fade + jnp.dot(w.astype(jnp.bfloat16), values, preferred_element_type=jnp.float32)

    def same(d):
        for upward in (True, False):
            owner = owner_of(upward, d)
            part = jnp.where(owner < y, A, B)
            attend(part, [(owner, part)])

    def late(d):
        attend(B, [(owner_of(True, d), A), (owner_of(False, d), A)])

    def both(part, d):
        for cut in range(CUTS):
            arrive(False, part, d, cut)
            arrive(True, part, d, cut)

        @pl.when(jnp.logical_and(jnp.logical_and(d == GO, part == B), jnp.logical_and(last_plane, first)))
        def _():
            pl.semaphore_signal(go, inc=1, device_id=twin, device_id_type=MESH)

    both(A, 1)
    both(B, 1)

    for part in (A, B):
        for j in range(NX):
            landed(q_copy, q_ends, q_recv, j, part, first)
        for g in range(SHARE):
            qs[part, g * BLK:(g + 1) * BLK, :] = qbuf[part, :, g * HD:(g + 1) * HD]

    attend(A, [(y, A)], 0)
    attend(B, [(y, A), (y, B)], BLK)

    def step(d, _):
        both(A, d)
        late(d - 1)
        both(B, d)
        same(d - 1)
        return 0

    lax.fori_loop(2, FAR, step, 0)
    late(FAR - 1)
    same(FAR - 1)
    for cut in range(CUTS):
        arrive(True, A, FAR, cut)
    far = owner_of(True, FAR)

    @pl.when(far < y)
    def _():
        attend(A, [(far, A)])

    def finish(part):
        o = acc[part] / total[part]
        for g in range(SHARE):
            obuf[part, :, g * HD:(g + 1) * HD] = o[g * BLK:(g + 1) * BLK].astype(jnp.bfloat16)
        begin(out_copy, out_ends, out_recv, part, jnp.logical_not(first))

    finish(A)
    for cut in range(CUTS):
        arrive(True, B, FAR, cut)
        arrive(False, B, FAR, cut)

    @pl.when(far < y)
    def _():
        attend(B, [(far, A)])

    @pl.when(far > y)
    def _():
        attend(B, [(far, A), (far, B)])

    finish(B)

    for part in (A, B):
        sent(kv_copy, part, first)
        sent(q_copy, part, first)
        for d in range(FAR):
            for upward in (True, False):
                @pl.when(needed(upward, part, d))
                def _():
                    for cut in range(CUTS):
                        ring(upward, part, d, cut).wait_send()
        sent(out_copy, part, jnp.logical_not(first))

    for part in (A, B):
        @pl.when(jnp.logical_not(first))
        def _():
            local(out_ends, out_recv, part).wait()

        for j in range(NX):
            def came():
                dst = out_ref.at[0, pl.ds(part * HALF, HALF), head(peers[j][1])]
                pltpu.make_async_remote_copy(
                    src_ref=obuf.at[part, pl.ds(0, HALF), :], dst_ref=dst,
                    send_sem=out_send.at[j, part], recv_sem=out_recv.at[j, part],
                    device_id=(out_pipe, at(peers[j][1], y)), device_id_type=MESH).wait_recv()

            if j == 0:
                pl.when(first)(came)
            else:
                came()


def shards(queries, keys_values):
    dma = pltpu.SemaphoreType.DMA
    bf16, f32 = jnp.bfloat16, jnp.float32
    return pl.pallas_call(
        kernel,
        out_shape=pltpu.VMEM(queries.shape, bf16),
        in_specs=[pl.BlockSpec(memory_space=pltpu.HBM), pl.BlockSpec(memory_space=pltpu.HBM)],
        out_specs=pl.BlockSpec(memory_space=pl.ANY),
        scratch_shapes=[
            pltpu.VMEM(keys_values.shape[1:], bf16),
            pltpu.VMEM((KVH, 2, 2, HALF, HD), bf16),
            pltpu.VMEM((NY, 2, 2, BLK, HD), bf16),
            pltpu.VMEM((2, BLK, WIDE), bf16),
            pltpu.VMEM((2, ROWS, HD), bf16),
            pltpu.VMEM((2, BLK, WIDE), bf16),
            pltpu.VMEM((2, ROWS, HD), f32),
            pltpu.VMEM((2, ROWS, HD), f32),
            pltpu.VMEM((2, ROWS, HD), f32),
            dma, dma((NX, 2)), dma((NX, 2)), dma((NX, 2)), dma((NX, 2)),
            dma((2, FAR, CUTS)), dma((2, FAR, CUTS)), dma((2, FAR, CUTS)), dma((2, FAR, CUTS)),
            dma((NX, 2)), dma((NX, 2)), pltpu.SemaphoreType.REGULAR,
        ],
        compiler_params=pltpu.CompilerParams(
            collective_id=0, has_side_effects=True, vmem_limit_bytes=48 * 1024 * 1024),
        cost_estimate=pl.CostEstimate(flops=3_500_000_000, bytes_accessed=4_000_000, transcendentals=3_400_000),
    )(pltpu.with_memory_space_constraint(queries, pltpu.HBM), pltpu.with_memory_space_constraint(keys_values, pltpu.HBM))


def solution(mesh):
    placed = (P("pipe", "ctx", None), P("pipe", "ctx", None, None))
    return jax.shard_map(
        shards, mesh=mesh, in_specs=placed, out_specs=P("pipe", "ctx", None), check_vma=False
    )
```

```python
import functools
import math

import jax
import jax.numpy as jnp
from jax import lax
from jax.experimental import pallas as pl
from jax.experimental.pallas import tpu as pltpu
from jax.sharding import PartitionSpec as P

HD = 128
KVH = 4
SHARE = 3
NSEQ = 2
NX = 4
NY = 8
FAR = NY // 2
CUTS = 2
HALF = 64
BLK = NX * HALF
ROWS = SHARE * BLK
CUT = BLK // CUTS
WIDE = SHARE * HD
GO = 2
NEG = -1e30
MESH = pl.DeviceIdType.MESH
A, B = 0, 1


def kernel(q_ref, kv_ref, out_ref, kvin, kvs, kvbuf, qbuf, qs, obuf, top, total, acc,
           load, kv_send, kv_recv, q_send, q_recv, up_send, up_recv, down_send, down_recv,
           out_send, out_recv, go):
    pipe = lax.axis_index("pipe")
    ctx = lax.axis_index("ctx")
    core = lax.rem(ctx, NSEQ)
    x = lax.rem(ctx // NSEQ, NX)
    y = ctx // (NSEQ * NX)
    npipe = lax.axis_size("pipe")
    nxt, prv = lax.rem(pipe + 1, npipe), lax.rem(pipe + npipe - 1, npipe)
    first = core == 1
    in_pipe = jnp.where(first, pipe, nxt)
    out_pipe = jnp.where(first, nxt, pipe)

    def at(px, py):
        return (py * NX + px) * NSEQ + core

    up = (pipe, at(x, lax.rem(y + 1, NY)))
    down = (pipe, at(x, lax.rem(y + NY - 1, NY)))
    twin = (pipe, (y * NX + x) * NSEQ + 1 - core)
    peers = [(lax.rem(x + j, NX), lax.rem(x + NX - j, NX)) for j in range(NX)]

    kv_in = pltpu.make_async_copy(kv_ref.at[0], kvin, load)
    kv_in.start()

    barrier = pltpu.get_barrier_semaphore()

    def greet(device):
        pl.semaphore_signal(barrier, inc=1, device_id=device, device_id_type=MESH)

    for j in range(1, NX):
        greet((pipe, at(peers[j][0], y)))
    greet(up)
    greet(down)
    greet(twin)
    for j in range(NX):
        greet((prv, at(peers[j][0], y)))

    def separate(part):
        for i in range(2):
            rows = kvin[part * HALF:(part + 1) * HALF, i, :]
            for h in range(KVH):
                kvs[h, part, i] = rows[:, h * HD:(h + 1) * HD]

    kv_in.wait()
    separate(A)
    pl.semaphore_wait(barrier, 2 * NX + 2)

    def place(px, part):
        return pl.ds(pl.multiple_of((px if part == A else NX - 1 - px) * HALF, HALF), HALF)

    def head(h):
        return pl.ds(pl.multiple_of(h * WIDE, HD), WIDE)

    def kv_ends(j, part):
        return kvs.at[peers[j][0], part], kvbuf.at[y, part, :, place(x, part), :]

    def q_ends(j, part):
        return q_ref.at[0, pl.ds(part * HALF, HALF), head(peers[j][0])], qbuf.at[part, place(x, part), :]

    def out_ends(j, part):
        return obuf.at[part, place(peers[j][0], part), :], out_ref.at[0, pl.ds(part * HALF, HALF), head(x)]

    def remote(ends, send, recv, j, part, to_pipe):
        src, dst = ends(j, part)
        return pltpu.make_async_remote_copy(
            src_ref=src, dst_ref=dst, send_sem=send.at[j, part], recv_sem=recv.at[j, part],
            device_id=(to_pipe, at(peers[j][0], y)), device_id_type=MESH)

    def local(ends, recv, part):
        src, dst = ends(0, part)
        return pltpu.make_async_copy(src, dst, recv.at[0, part])

    kv_copy = lambda j, part: remote(kv_ends, kv_send, kv_recv, j, part, in_pipe)
    q_copy = lambda j, part: remote(q_ends, q_send, q_recv, j, part, in_pipe)
    out_copy = lambda j, part: remote(out_ends, out_send, out_recv, j, part, out_pipe)

    def begin(copy, ends, recv, part, stays):
        @pl.when(stays)
        def _():
            local(ends, recv, part).start()

        @pl.when(jnp.logical_not(stays))
        def _():
            copy(0, part).start()

        for j in (1, 3, 2):
            copy(j, part).start()

    def landed(copy, ends, recv, j, part, stays):
        if j > 0:
            copy(j, part).wait_recv()
            return

        @pl.when(stays)
        def _():
            local(ends, recv, part).wait()

        @pl.when(jnp.logical_not(stays))
        def _():
            copy(0, part).wait_recv()

    def sent(copy, part, stays):
        @pl.when(jnp.logical_not(stays))
        def _():
            copy(0, part).wait_send()

        for j in (1, 3, 2):
            copy(j, part).wait_send()

    begin(kv_copy, kv_ends, kv_recv, A, first)
    separate(B)
    begin(kv_copy, kv_ends, kv_recv, B, first)
    begin(q_copy, q_ends, q_recv, A, first)
    begin(q_copy, q_ends, q_recv, B, first)

    top[...] = jnp.full_like(top, NEG)
    total[...] = jnp.zeros_like(total)
    acc[...] = jnp.zeros_like(acc)

    def owner_of(upward, d):
        return lax.rem(y + NY - d, NY) if upward else lax.rem(y + d, NY)

    def ring(upward, part, d, cut):
        slot = kvbuf.at[owner_of(upward, d), part, :, pl.ds(cut * CUT, CUT), :]
        send, recv = (up_send, up_recv) if upward else (down_send, down_recv)
        return pltpu.make_async_remote_copy(
            src_ref=slot, dst_ref=slot, send_sem=send.at[part, d, cut], recv_sem=recv.at[part, d, cut],
            device_id=up if upward else down, device_id_type=MESH)

    def travels(upward, part, owner, d):
        if part == A:
            return d <= (FAR if upward else FAR - 1)
        if upward:
            return jnp.logical_and(owner > FAR, d <= FAR)
        return jnp.logical_and(owner >= d, d <= jnp.where(owner == FAR, FAR, FAR - 1))

    def needed(upward, part, d):
        return travels(upward, part, owner_of(upward, d), d + 1)

    def arrive(upward, part, d, cut):
        owner = owner_of(upward, d)
        slot = kvbuf.at[owner, part, :, pl.ds(cut * CUT, CUT), :]
        send, recv = (up_send, up_recv) if upward else (down_send, down_recv)

        @pl.when(travels(upward, part, owner, d))
        def _():
            pltpu.make_async_remote_copy(
                src_ref=slot, dst_ref=slot, send_sem=send.at[part, d - 1, cut], recv_sem=recv.at[part, d - 1, cut],
                device_id=up if upward else down, device_id_type=MESH).wait_recv()

        @pl.when(needed(upward, part, d))
        def _():
            ring(upward, part, d, cut).start()

    last_plane = pipe == npipe - 1

    @pl.when(jnp.logical_and(last_plane, jnp.logical_not(first)))
    def _():
        pl.semaphore_wait(go, 1)

    for part, j in ((A, 0), (B, 0), (A, 1), (A, 3), (A, 2), (B, 1), (B, 3), (B, 2)):
        landed(kv_copy, kv_ends, kv_recv, j, part, first)
        frm = peers[j][1]
        piece = kvbuf.at[y, part, :, place(frm, part), :]
        cut = (frm if part == A else NX - 1 - frm) // (NX // CUTS)
        for upward in (True, False):
            @pl.when(needed(upward, part, 0))
            def _():
                pltpu.make_async_remote_copy(
                    src_ref=piece, dst_ref=piece,
                    send_sem=(up_send if upward else down_send).at[part, 0, cut],
                    recv_sem=(up_recv if upward else down_recv).at[part, 0, cut],
                    device_id=up if upward else down, device_id_type=MESH).start()

    factor = math.log2(math.e) / math.sqrt(HD)

    def attend(rows, blocks, shift=None):
        keys = jnp.concatenate([kvbuf[o, p, 0] for o, p in blocks], axis=0)
        values = jnp.concatenate([kvbuf[o, p, 1] for o, p in blocks], axis=0)
        count = len(blocks) * BLK
        s = lax.dot_general(qs[rows], keys, (((1,), (1,)), ((), ())), preferred_element_type=jnp.float32)
        if shift is not None:
            q_at = lax.broadcasted_iota(jnp.int32, (SHARE, BLK, count), 1).reshape(ROWS, count)
            k_at = lax.broadcasted_iota(jnp.int32, (ROWS, count), 1)
            s = jnp.where(k_at <= q_at + shift, s, NEG)
        old = top[rows]
        new = jnp.maximum(old, jnp.max(s, axis=1, keepdims=True))
        fade = jnp.exp2((old - new) * factor)
        w = jnp.exp2((s - jnp.concatenate([new] * (count // HD), axis=1)) * factor)
        top[rows] = new
        total[rows] = total[rows] * fade + jnp.sum(w, axis=1, keepdims=True)
        acc[rows] = acc[rows] * fade + jnp.dot(w.astype(jnp.bfloat16), values, preferred_element_type=jnp.float32)

    def same(d):
        for upward in (True, False):
            owner = owner_of(upward, d)
            part = jnp.where(owner < y, A, B)
            attend(part, [(owner, part)])

    def late(d):
        attend(B, [(owner_of(True, d), A), (owner_of(False, d), A)])

    def both(part, d):
        for cut in range(CUTS):
            arrive(False, part, d, cut)
            arrive(True, part, d, cut)

        @pl.when(jnp.logical_and(jnp.logical_and(d == GO, part == B), jnp.logical_and(last_plane, first)))
        def _():
            pl.semaphore_signal(go, inc=1, device_id=twin, device_id_type=MESH)

    both(A, 1)
    both(B, 1)

    for part in (A, B):
        for j in range(NX):
            landed(q_copy, q_ends, q_recv, j, part, first)
        for g in range(SHARE):
            qs[part, g * BLK:(g + 1) * BLK, :] = qbuf[part, :, g * HD:(g + 1) * HD]

    attend(A, [(y, A)], 0)
    attend(B, [(y, A), (y, B)], BLK)

    def step(d, _):
        both(A, d)
        late(d - 1)
        both(B, d)
        same(d - 1)
        return 0

    lax.fori_loop(2, FAR, step, 0)
    late(FAR - 1)
    same(FAR - 1)
    for cut in range(CUTS):
        arrive(True, A, FAR, cut)
    far = owner_of(True, FAR)

    @pl.when(far < y)
    def _():
        attend(A, [(far, A)])

    def finish(part):
        o = acc[part] / total[part]
        for g in range(SHARE):
            obuf[part, :, g * HD:(g + 1) * HD] = o[g * BLK:(g + 1) * BLK].astype(jnp.bfloat16)
        begin(out_copy, out_ends, out_recv, part, jnp.logical_not(first))

    finish(A)
    attend(B, [(far, A)])
    for cut in range(CUTS):
        arrive(False, B, FAR, cut)
        arrive(True, B, FAR, cut)

    @pl.when(far > y)
    def _():
        attend(B, [(far, B)])

    finish(B)

    for part in (A, B):
        sent(kv_copy, part, first)
        sent(q_copy, part, first)
        for d in range(FAR):
            for upward in (True, False):
                @pl.when(needed(upward, part, d))
                def _():
                    for cut in range(CUTS):
                        ring(upward, part, d, cut).wait_send()
        sent(out_copy, part, jnp.logical_not(first))

    for part in (A, B):
        @pl.when(jnp.logical_not(first))
        def _():
            local(out_ends, out_recv, part).wait()

        for j in range(NX):
            def came():
                dst = out_ref.at[0, pl.ds(part * HALF, HALF), head(peers[j][1])]
                pltpu.make_async_remote_copy(
                    src_ref=obuf.at[part, pl.ds(0, HALF), :], dst_ref=dst,
                    send_sem=out_send.at[j, part], recv_sem=out_recv.at[j, part],
                    device_id=(out_pipe, at(peers[j][1], y)), device_id_type=MESH).wait_recv()

            if j == 0:
                pl.when(first)(came)
            else:
                came()


def shards(queries, keys_values):
    dma = pltpu.SemaphoreType.DMA
    bf16, f32 = jnp.bfloat16, jnp.float32
    return pl.pallas_call(
        kernel,
        out_shape=pltpu.VMEM(queries.shape, bf16),
        in_specs=[pl.BlockSpec(memory_space=pltpu.HBM), pl.BlockSpec(memory_space=pltpu.HBM)],
        out_specs=pl.BlockSpec(memory_space=pl.ANY),
        scratch_shapes=[
            pltpu.VMEM(keys_values.shape[1:], bf16),
            pltpu.VMEM((KVH, 2, 2, HALF, HD), bf16),
            pltpu.VMEM((NY, 2, 2, BLK, HD), bf16),
            pltpu.VMEM((2, BLK, WIDE), bf16),
            pltpu.VMEM((2, ROWS, HD), bf16),
            pltpu.VMEM((2, BLK, WIDE), bf16),
            pltpu.VMEM((2, ROWS, HD), f32),
            pltpu.VMEM((2, ROWS, HD), f32),
            pltpu.VMEM((2, ROWS, HD), f32),
            dma, dma((NX, 2)), dma((NX, 2)), dma((NX, 2)), dma((NX, 2)),
            dma((2, FAR, CUTS)), dma((2, FAR, CUTS)), dma((2, FAR, CUTS)), dma((2, FAR, CUTS)),
            dma((NX, 2)), dma((NX, 2)), pltpu.SemaphoreType.REGULAR,
        ],
        compiler_params=pltpu.CompilerParams(
            collective_id=0, has_side_effects=True, vmem_limit_bytes=48 * 1024 * 1024),
        cost_estimate=pl.CostEstimate(flops=3_500_000_000, bytes_accessed=4_000_000, transcendentals=3_400_000),
    )(pltpu.with_memory_space_constraint(queries, pltpu.HBM), pltpu.with_memory_space_constraint(keys_values, pltpu.HBM))


def solution(mesh):
    placed = (P("pipe", "ctx", None), P("pipe", "ctx", None, None))
    return jax.shard_map(
        shards, mesh=mesh, in_specs=placed, out_specs=P("pipe", "ctx", None), check_vma=False
    )
```

```python
import functools
import math

import jax
import jax.numpy as jnp
from jax import lax
from jax.experimental import pallas as pl
from jax.experimental.pallas import tpu as pltpu
from jax.sharding import PartitionSpec as P

HD = 128
KVH = 4
SHARE = 3
NSEQ = 2
NX = 4
NY = 8
FAR = NY // 2
CUTS = 2
HALF = 64
BLK = NX * HALF
ROWS = SHARE * BLK
CUT = BLK // CUTS
WIDE = SHARE * HD
GO = 2
NEG = -1e30
MESH = pl.DeviceIdType.MESH
A, B = 0, 1


def kernel(q_ref, kv_ref, out_ref, kvin, kvs, kvbuf, qbuf, qs, obuf, top, total, acc,
           load, kv_send, kv_recv, q_send, q_recv, up_send, up_recv, down_send, down_recv,
           out_send, out_recv, go):
    pipe = lax.axis_index("pipe")
    ctx = lax.axis_index("ctx")
    core = lax.rem(ctx, NSEQ)
    x = lax.rem(ctx // NSEQ, NX)
    y = ctx // (NSEQ * NX)
    npipe = lax.axis_size("pipe")
    nxt, prv = lax.rem(pipe + 1, npipe), lax.rem(pipe + npipe - 1, npipe)
    first = core == 1
    in_pipe = jnp.where(first, pipe, nxt)
    out_pipe = jnp.where(first, nxt, pipe)

    def at(px, py):
        return (py * NX + px) * NSEQ + core

    up = (pipe, at(x, lax.rem(y + 1, NY)))
    down = (pipe, at(x, lax.rem(y + NY - 1, NY)))
    twin = (pipe, (y * NX + x) * NSEQ + 1 - core)
    peers = [(lax.rem(x + j, NX), lax.rem(x + NX - j, NX)) for j in range(NX)]

    kv_in = pltpu.make_async_copy(kv_ref.at[0], kvin, load)
    kv_in.start()

    barrier = pltpu.get_barrier_semaphore()

    def greet(device):
        pl.semaphore_signal(barrier, inc=1, device_id=device, device_id_type=MESH)

    for j in range(1, NX):
        greet((pipe, at(peers[j][0], y)))
    greet(up)
    greet(down)
    greet(twin)
    for j in range(NX):
        greet((prv, at(peers[j][0], y)))

    def separate(part):
        for i in range(2):
            rows = kvin[part * HALF:(part + 1) * HALF, i, :]
            for h in range(KVH):
                kvs[h, part, i] = rows[:, h * HD:(h + 1) * HD]

    kv_in.wait()
    separate(A)
    pl.semaphore_wait(barrier, 2 * NX + 2)

    def place(px, part):
        return pl.ds(pl.multiple_of((px if part == A else NX - 1 - px) * HALF, HALF), HALF)

    def head(h):
        return pl.ds(pl.multiple_of(h * WIDE, HD), WIDE)

    def kv_ends(j, part):
        return kvs.at[peers[j][0], part], kvbuf.at[y, part, :, place(x, part), :]

    def q_ends(j, part):
        return q_ref.at[0, pl.ds(part * HALF, HALF), head(peers[j][0])], qbuf.at[part, place(x, part), :]

    def out_ends(j, part):
        return obuf.at[part, place(peers[j][0], part), :], out_ref.at[0, pl.ds(part * HALF, HALF), head(x)]

    def remote(ends, send, recv, j, part, to_pipe):
        src, dst = ends(j, part)
        return pltpu.make_async_remote_copy(
            src_ref=src, dst_ref=dst, send_sem=send.at[j, part], recv_sem=recv.at[j, part],
            device_id=(to_pipe, at(peers[j][0], y)), device_id_type=MESH)

    def local(ends, recv, part):
        src, dst = ends(0, part)
        return pltpu.make_async_copy(src, dst, recv.at[0, part])

    kv_copy = lambda j, part: remote(kv_ends, kv_send, kv_recv, j, part, in_pipe)
    q_copy = lambda j, part: remote(q_ends, q_send, q_recv, j, part, in_pipe)
    out_copy = lambda j, part: remote(out_ends, out_send, out_recv, j, part, out_pipe)

    def begin(copy, ends, recv, part, stays, order=(1, 3, 2)):
        @pl.when(stays)
        def _():
            local(ends, recv, part).start()

        @pl.when(jnp.logical_not(stays))
        def _():
            copy(0, part).start()

        for j in order:
            copy(j, part).start()

    def landed(copy, ends, recv, j, part, stays):
        if j > 0:
            copy(j, part).wait_recv()
            return

        @pl.when(stays)
        def _():
            local(ends, recv, part).wait()

        @pl.when(jnp.logical_not(stays))
        def _():
            copy(0, part).wait_recv()

    def sent(copy, part, stays):
        @pl.when(jnp.logical_not(stays))
        def _():
            copy(0, part).wait_send()

        for j in (1, 3, 2):
            copy(j, part).wait_send()

    begin(kv_copy, kv_ends, kv_recv, A, first)
    separate(B)
    begin(kv_copy, kv_ends, kv_recv, B, first)
    begin(q_copy, q_ends, q_recv, A, first)
    begin(q_copy, q_ends, q_recv, B, first)

    top[...] = jnp.full_like(top, NEG)
    total[...] = jnp.zeros_like(total)
    acc[...] = jnp.zeros_like(acc)

    def owner_of(upward, d):
        return lax.rem(y + NY - d, NY) if upward else lax.rem(y + d, NY)

    def ring(upward, part, d, cut):
        slot = kvbuf.at[owner_of(upward, d), part, :, pl.ds(cut * CUT, CUT), :]
        send, recv = (up_send, up_recv) if upward else (down_send, down_recv)
        return pltpu.make_async_remote_copy(
            src_ref=slot, dst_ref=slot, send_sem=send.at[part, d, cut], recv_sem=recv.at[part, d, cut],
            device_id=up if upward else down, device_id_type=MESH)

    def travels(upward, part, owner, d):
        if part == A:
            return d <= (FAR if upward else FAR - 1)
        if upward:
            return jnp.logical_and(owner > FAR, d <= FAR)
        return jnp.logical_and(owner >= d, d <= jnp.where(owner == FAR, FAR, FAR - 1))

    def needed(upward, part, d):
        return travels(upward, part, owner_of(upward, d), d + 1)

    def arrive(upward, part, d, cut):
        owner = owner_of(upward, d)
        slot = kvbuf.at[owner, part, :, pl.ds(cut * CUT, CUT), :]
        send, recv = (up_send, up_recv) if upward else (down_send, down_recv)

        @pl.when(travels(upward, part, owner, d))
        def _():
            pltpu.make_async_remote_copy(
                src_ref=slot, dst_ref=slot, send_sem=send.at[part, d - 1, cut], recv_sem=recv.at[part, d - 1, cut],
                device_id=up if upward else down, device_id_type=MESH).wait_recv()

        @pl.when(needed(upward, part, d))
        def _():
            ring(upward, part, d, cut).start()

    last_plane = pipe == npipe - 1

    @pl.when(jnp.logical_and(last_plane, jnp.logical_not(first)))
    def _():
        pl.semaphore_wait(go, 1)

    for part, j in ((A, 0), (B, 0), (A, 1), (A, 3), (A, 2), (B, 1), (B, 3), (B, 2)):
        landed(kv_copy, kv_ends, kv_recv, j, part, first)
        frm = peers[j][1]
        piece = kvbuf.at[y, part, :, place(frm, part), :]
        cut = (frm if part == A else NX - 1 - frm) // (NX // CUTS)
        for upward in (True, False):
            @pl.when(needed(upward, part, 0))
            def _():
                pltpu.make_async_remote_copy(
                    src_ref=piece, dst_ref=piece,
                    send_sem=(up_send if upward else down_send).at[part, 0, cut],
                    recv_sem=(up_recv if upward else down_recv).at[part, 0, cut],
                    device_id=up if upward else down, device_id_type=MESH).start()

    factor = math.log2(math.e) / math.sqrt(HD)

    def attend(rows, blocks, shift=None):
        keys = jnp.concatenate([kvbuf[o, p, 0] for o, p in blocks], axis=0)
        values = jnp.concatenate([kvbuf[o, p, 1] for o, p in blocks], axis=0)
        count = len(blocks) * BLK
        s = lax.dot_general(qs[rows], keys, (((1,), (1,)), ((), ())), preferred_element_type=jnp.float32)
        if shift is not None:
            q_at = lax.broadcasted_iota(jnp.int32, (SHARE, BLK, count), 1).reshape(ROWS, count)
            k_at = lax.broadcasted_iota(jnp.int32, (ROWS, count), 1)
            s = jnp.where(k_at <= q_at + shift, s, NEG)
        old = top[rows]
        new = jnp.maximum(old, jnp.max(s, axis=1, keepdims=True))
        fade = jnp.exp2((old - new) * factor)
        w = jnp.exp2((s - jnp.concatenate([new] * (count // HD), axis=1)) * factor)
        top[rows] = new
        total[rows] = total[rows] * fade + jnp.sum(w, axis=1, keepdims=True)
        acc[rows] = acc[rows] * fade + jnp.dot(w.astype(jnp.bfloat16), values, preferred_element_type=jnp.float32)

    def same(d):
        for upward in (True, False):
            owner = owner_of(upward, d)
            part = jnp.where(owner < y, A, B)
            attend(part, [(owner, part)])

    def late(d):
        attend(B, [(owner_of(True, d), A), (owner_of(False, d), A)])

    def both(part, d):
        for cut in range(CUTS):
            arrive(False, part, d, cut)
            arrive(True, part, d, cut)

        @pl.when(jnp.logical_and(jnp.logical_and(d == GO, part == B), jnp.logical_and(last_plane, first)))
        def _():
            pl.semaphore_signal(go, inc=1, device_id=twin, device_id_type=MESH)

    both(A, 1)
    both(B, 1)

    for part in (A, B):
        for j in range(NX):
            landed(q_copy, q_ends, q_recv, j, part, first)
        for g in range(SHARE):
            qs[part, g * BLK:(g + 1) * BLK, :] = qbuf[part, :, g * HD:(g + 1) * HD]

    attend(A, [(y, A)], 0)
    attend(B, [(y, A), (y, B)], BLK)

    def step(d, _):
        both(A, d)
        late(d - 1)
        both(B, d)
        same(d - 1)
        return 0

    lax.fori_loop(2, FAR, step, 0)
    late(FAR - 1)
    same(FAR - 1)
    for cut in range(CUTS):
        arrive(True, A, FAR, cut)
    far = owner_of(True, FAR)

    @pl.when(far < y)
    def _():
        attend(A, [(far, A)])

    def finish(part):
        o = acc[part] / total[part]
        for g in range(SHARE):
            obuf[part, :, g * HD:(g + 1) * HD] = o[g * BLK:(g + 1) * BLK].astype(jnp.bfloat16)
        begin(out_copy, out_ends, out_recv, part, jnp.logical_not(first), (2, 1, 3))

    finish(A)
    attend(B, [(far, A)])
    for cut in range(CUTS):
        arrive(False, B, FAR, cut)
        arrive(True, B, FAR, cut)

    @pl.when(far > y)
    def _():
        attend(B, [(far, B)])

    finish(B)

    for part in (A, B):
        sent(kv_copy, part, first)
        sent(q_copy, part, first)
        for d in range(FAR):
            for upward in (True, False):
                @pl.when(needed(upward, part, d))
                def _():
                    for cut in range(CUTS):
                        ring(upward, part, d, cut).wait_send()
        sent(out_copy, part, jnp.logical_not(first))

    for part in (A, B):
        @pl.when(jnp.logical_not(first))
        def _():
            local(out_ends, out_recv, part).wait()

        for j in range(NX):
            def came():
                dst = out_ref.at[0, pl.ds(part * HALF, HALF), head(peers[j][1])]
                pltpu.make_async_remote_copy(
                    src_ref=obuf.at[part, pl.ds(0, HALF), :], dst_ref=dst,
                    send_sem=out_send.at[j, part], recv_sem=out_recv.at[j, part],
                    device_id=(out_pipe, at(peers[j][1], y)), device_id_type=MESH).wait_recv()

            if j == 0:
                pl.when(first)(came)
            else:
                came()


def shards(queries, keys_values):
    dma = pltpu.SemaphoreType.DMA
    bf16, f32 = jnp.bfloat16, jnp.float32
    return pl.pallas_call(
        kernel,
        out_shape=pltpu.VMEM(queries.shape, bf16),
        in_specs=[pl.BlockSpec(memory_space=pltpu.HBM), pl.BlockSpec(memory_space=pltpu.HBM)],
        out_specs=pl.BlockSpec(memory_space=pl.ANY),
        scratch_shapes=[
            pltpu.VMEM(keys_values.shape[1:], bf16),
            pltpu.VMEM((KVH, 2, 2, HALF, HD), bf16),
            pltpu.VMEM((NY, 2, 2, BLK, HD), bf16),
            pltpu.VMEM((2, BLK, WIDE), bf16),
            pltpu.VMEM((2, ROWS, HD), bf16),
            pltpu.VMEM((2, BLK, WIDE), bf16),
            pltpu.VMEM((2, ROWS, HD), f32),
            pltpu.VMEM((2, ROWS, HD), f32),
            pltpu.VMEM((2, ROWS, HD), f32),
            dma, dma((NX, 2)), dma((NX, 2)), dma((NX, 2)), dma((NX, 2)),
            dma((2, FAR, CUTS)), dma((2, FAR, CUTS)), dma((2, FAR, CUTS)), dma((2, FAR, CUTS)),
            dma((NX, 2)), dma((NX, 2)), pltpu.SemaphoreType.REGULAR,
        ],
        compiler_params=pltpu.CompilerParams(
            collective_id=0, has_side_effects=True, vmem_limit_bytes=48 * 1024 * 1024),
        cost_estimate=pl.CostEstimate(flops=3_500_000_000, bytes_accessed=4_000_000, transcendentals=3_400_000),
    )(pltpu.with_memory_space_constraint(queries, pltpu.HBM), pltpu.with_memory_space_constraint(keys_values, pltpu.HBM))


def solution(mesh):
    placed = (P("pipe", "ctx", None), P("pipe", "ctx", None, None))
    return jax.shard_map(
        shards, mesh=mesh, in_specs=placed, out_specs=P("pipe", "ctx", None), check_vma=False
    )
```
